256 devices in a mesh: grp: 4 (over z_hi, core), cond: 16 (over z_lo, x), val: 4 (over y).
Axes of the slice: x: 4, y: 4, z: 8 (z_hi: 2, z_lo: 4; z = z_hi * 4 + z_lo), core: 2. Of those that a mesh axis runs over, the one named last changes fastest.
Arguments:
- screened: bfloat16 [8192, 8192], P('cond', ('grp', 'val')), may hold values from -0.0625 to 0.0625
- valence: bfloat16 [8192, 256], P(('grp', 'val')), may hold values from -6 to 6
- first_band: int32 [512], replicated, may hold values from 0 to 255
- second_band: int32 [512], replicated, may hold values from 0 to 255
- conduction: bfloat16 [512, 8192], P('cond'), may hold values from -6 to 6
- partners: int32 [4, 16, 4], P('grp', 'cond'), may hold values from -1 to 15, as said below
Outputs:
- kernel: float32 [4, 16, 4, 1024, 512], P('grp', 'cond', None, None, 'val')
The draws below stay inside these ranges and needn't reach their ends.
Inputs may be any that keep to these rules, and one draw needn't show every extreme that they name: partners[g, a, s] is -1 (empty slot) or a block b with a <= b; for every a, each b from a to 15 stands exactly once in partners[:, a, :]; in conduction row 0 some groups fill all 4 slots.
All inputs are finite; a program needn't handle non-finite values.
Results may differ from the reference program's by a relative error of at most 0.0049.
Values may be sent and summed in bfloat16 or wider, within the bound.
A program may use at most 64 MiB of HBM per device.

```python
import math
import jax
import jax.numpy as jnp
from jax import lax

NR = 8192
NV = 256
NCB = 32
NC = 512
VP = 512
SLOTS = 4
N_GRP = 4
N_COND = 16


def draw_partners(key, part):
    key = jax.random.fold_in(key, 7)
    blocks = N_COND
    groups = N_GRP
    slot_count = SLOTS
    row_keys = jax.random.split(key, blocks)

    def one_row(row_key, row_index):
        order_key, start_key = jax.random.split(row_key)
        shuffled = jax.random.permutation(order_key, blocks).astype(jnp.int32)
        usable = shuffled >= row_index
        position = jnp.arange(blocks, dtype=jnp.int32)
        ordering = jnp.argsort(jnp.where(usable, 0, 1) * blocks + position)
        ordered = shuffled[ordering]
        live_count = blocks - row_index
        offset = jax.random.randint(start_key, (), 0, groups)
        target_group = (offset + position) % groups
        target_slot = position // groups
        values = jnp.where(position < live_count, ordered, -1).astype(jnp.int32)
        layout = jnp.full((groups, slot_count), -1, jnp.int32)
        return layout.at[target_group, target_slot].set(values)
    tables = jax.vmap(one_row)(row_keys, jnp.arange(blocks, dtype=jnp.int32))
    return jnp.transpose(tables, (1, 0, 2))


def with_ends(values, key, least, largest):
    extent = values.shape
    place = [jax.random.randint(jax.random.fold_in(key, axis), (), 0, extent[axis]) for axis in range(len(extent))]
    values = values.at[tuple(place)].set(least)
    longest = extent.index(max(extent))
    place[longest] = (place[longest] + 1) % extent[longest]
    return values.at[tuple(place)].set(largest)


def shard_levels(rng, dims, cuts, low, largest):
    level = 1.0
    for axis_at, parts in cuts:
        steps = jax.random.uniform(jax.random.fold_in(jax.random.fold_in(rng, 6), axis_at), (parts,), jnp.float32, low / len(cuts), largest / len(cuts))
        level = level * jnp.repeat(jnp.exp(steps), dims[axis_at] // parts).reshape((-1,) + (1,) * (len(dims) - 1 - axis_at))
    return level


def scatter_about(stream_key, dims, width, bound, shards=(), held_as=jnp.bfloat16):
    drawn = width * jax.random.normal(stream_key, dims, jnp.float32)
    if shards:
        drawn = drawn * shard_levels(stream_key, dims, shards, -0.22, 0.18)
    return jnp.clip(drawn, -bound, bound).astype(held_as)


def setup_inputs(seed: int = 0) -> dict:
    streams_of = jax.random.split(jax.random.key(seed), 7)
    return {
        "screened": scatter_about(streams_of[0], (NR, NR), NR ** -0.5, 0.0625, ((0, 16), (1, 16))),
        "valence": scatter_about(streams_of[1], (NR, NV), 1.0, 6.0, ((0, 16),)),
        "first_band": with_ends(jax.random.randint(streams_of[2], (VP,), 0, NV), jax.random.fold_in(streams_of[2], 1), 0, NV - 1).astype(jnp.int32),
        "second_band": with_ends(jax.random.randint(streams_of[3], (VP,), 0, NV), jax.random.fold_in(streams_of[3], 1), 0, NV - 1).astype(jnp.int32),
        "conduction": scatter_about(streams_of[4], (NC, NR), 1.0, 6.0, ((0, 16),)),
        "partners": draw_partners(jax.random.fold_in(streams_of[6], 71), 0),
    }


def slot_kernel(conduction, mixed_wide, row_block, partner):
    upper = lax.dynamic_slice_in_dim(conduction, (row_block * NCB).astype(jnp.int32), NCB, 0).astype(jnp.float32)
    lower = lax.dynamic_slice_in_dim(conduction, (jnp.maximum(partner, 0) * NCB).astype(jnp.int32), NCB, 0).astype(jnp.float32)
    density = (upper[:, None, :] * lower[None, :, :]).reshape(NCB * NCB, NR).astype(jnp.bfloat16)
    density = lax.optimization_barrier(density).astype(jnp.float32)
    return jnp.dot(density, mixed_wide, precision=lax.Precision.HIGHEST) / math.sqrt(NR)

def reference(screened, valence, first_band, second_band, conduction, partners):
    first_cols = valence[:, first_band].astype(jnp.float32)
    second_cols = valence[:, second_band].astype(jnp.float32)
    pair_density = (first_cols * second_cols).astype(jnp.bfloat16)
    mixed = jnp.dot(screened.astype(jnp.float32), pair_density.astype(jnp.float32), precision=lax.Precision.HIGHEST)
    mixed = lax.optimization_barrier(mixed.astype(jnp.bfloat16)).astype(jnp.float32)
    flat_partners = partners.reshape(-1).astype(jnp.int32)
    slot_ids = jnp.arange(flat_partners.shape[0], dtype=jnp.int32)
    row_blocks = slot_ids // SLOTS % N_COND

    def one_slot(pieces):
        row_block, partner = pieces
        blank = jnp.zeros((NCB * NCB, VP), jnp.float32)
        return lax.cond(partner >= 0, lambda unused: slot_kernel(conduction, mixed, row_block, partner), lambda unused: blank, 0)
    blocks = lax.map(one_slot, (row_blocks, flat_partners))
    return blocks.reshape(N_GRP, N_COND, SLOTS, NCB * NCB, VP)
```

```python
import math

import jax
import jax.numpy as jnp
from jax import lax
from jax.experimental import pallas as pl
from jax.experimental.pallas import tpu as pltpu
from jax.sharding import PartitionSpec as P

CHUNK = 1024


def blocks_kernel(partners_ref, left_ref, right_ref, mixed_ref, out_ref):
    bands = left_ref.shape[0]
    points = left_ref.shape[1]
    slots = right_ref.shape[0] // bands
    out_ref[...] = jnp.zeros_like(out_ref)

    def step(i, carry):
        part = pl.ds(pl.multiple_of(i * CHUNK, CHUNK), CHUNK)
        mixed = mixed_ref[part, :]
        for s in range(slots):
            right = right_ref[s * bands : (s + 1) * bands, part]
            rows = [
                jnp.broadcast_to(left_ref[x : x + 1, part], right.shape) * right
                for x in range(bands)
            ]
            density = jnp.concatenate(rows, 0)
            out_ref[s] += jnp.dot(density, mixed, preferred_element_type=jnp.float32)
        return carry

    lax.fori_loop(0, points // CHUNK, step, 0)
    for s in range(slots):
        scale = jnp.where(partners_ref[s] >= 0, 1.0 / math.sqrt(points), 0.0)
        out_ref[s] = out_ref[s] * scale


def on_device(screened, valence, first_band, second_band, conduction, partners):
    band_count = valence.shape[1]
    bands = conduction.shape[0]
    points = conduction.shape[1]
    band_index = lax.broadcasted_iota(jnp.int32, (band_count, first_band.shape[0]), 0)
    first_cols = jnp.dot(
        valence,
        (band_index == first_band[None, :]).astype(jnp.bfloat16),
        preferred_element_type=jnp.float32,
    )
    second_cols = jnp.dot(
        valence,
        (band_index == second_band[None, :]).astype(jnp.bfloat16),
        preferred_element_type=jnp.float32,
    )
    pair_density = (first_cols * second_cols).astype(jnp.bfloat16)
    partial_mix = jnp.dot(screened, pair_density, preferred_element_type=jnp.float32)
    own = lax.psum_scatter(partial_mix, "val", scatter_dimension=1, tiled=True)
    own = lax.psum(own, "grp")
    mixed = lax.all_gather(own.astype(jnp.bfloat16), "cond", axis=0, tiled=True)
    every = lax.all_gather(conduction, "cond", axis=0, tiled=True)
    owned = partners.reshape(-1)
    right = jnp.concatenate(
        [
            lax.dynamic_slice_in_dim(every, jnp.maximum(owned[s], 0) * bands, bands, 0)
            for s in range(owned.shape[0])
        ],
        0,
    )
    vmem = pl.BlockSpec(memory_space=pltpu.VMEM)
    kernel = pl.pallas_call(
        blocks_kernel,
        out_shape=jax.ShapeDtypeStruct(
            (owned.shape[0], bands * bands, mixed.shape[1]), jnp.float32
        ),
        in_specs=[pl.BlockSpec(memory_space=pltpu.SMEM), vmem, vmem, vmem],
        out_specs=vmem,
        compiler_params=pltpu.CompilerParams(vmem_limit_bytes=48 * 2**20),
    )(owned, conduction, right, mixed)
    return kernel.reshape((1, 1) + kernel.shape)


def solution(mesh):
    in_specs = (
        P("cond", ("grp", "val")),
        P(("grp", "val"), None),
        P(),
        P(),
        P("cond", None),
        P("grp", "cond", None),
    )
    out_specs = P("grp", "cond", None, None, "val")
    return jax.shard_map(
        on_device, mesh=mesh, in_specs=in_specs, out_specs=out_specs, check_vma=False
    )
```

```python
import math

import jax
import jax.numpy as jnp
from jax import lax
from jax.experimental import pallas as pl
from jax.experimental.pallas import tpu as pltpu
from jax.sharding import PartitionSpec as P

MESH = pl.DeviceIdType.MESH
BF16 = jnp.bfloat16
F32 = jnp.float32
SIDE = 4
BANDS = 32
SLOTS = 4
POINTS = 8192
PAIRS = 512
OWN_PAIRS = 128
HALF_ROWS = 256
PIECE = 1024


def whole_kernel(
    partners_ref,
    first_ref,
    second_ref,
    screened_ref,
    valence_ref,
    conduction_ref,
    out_ref,
    left,
    scr,
    val,
    dens,
    sums,
    tosend,
    parts,
    zout,
    zin,
    gath,
    mix,
    sel,
    loc_sem,
    pair_send,
    pair_recv,
    y_send,
    y_recv,
    z_send,
    z_recv,
    ga_send,
    ga_recv,
    gb_send,
    gb_recv,
    gs_send,
    gs_recv,
    ma_send,
    ma_recv,
    mb_send,
    mb_recv,
    ms_send,
    ms_recv,
    sel_send,
    sel_recv,
):
    grp = lax.axis_index("grp")
    cond = lax.axis_index("cond")
    y = lax.axis_index("val")
    core = lax.rem(grp, 2)
    x = lax.rem(cond, SIDE)
    zlo = cond // SIDE
    z = (grp // 2) * SIDE + zlo
    par = lax.rem(x, 2)

    def device(px, py, pz, pcore):
        px = lax.rem(px + SIDE, SIDE)
        py = lax.rem(py + SIDE, SIDE)
        pz = lax.rem(pz + 2 * SIDE, 2 * SIDE)
        return ((pz // SIDE) * 2 + pcore, lax.rem(pz, SIDE) * SIDE + px, py)

    sibling = device(x, y, z, 1 - core)
    opposite = device(x, y, z + SIDE, core)

    def y_peer(j):
        return device(x, y + j, z, core)

    def z_step(j, up):
        return (0, 1, up * 4 - 2, -1)[j]

    pa = x * (1 - core) + zlo * core
    pb = zlo * (1 - core) + x * core

    def peer_a(j):
        return device(x + j * (1 - core), y, z + z_step(j, par) * core, core)

    def peer_b(j, up):
        return device(x + j * core, y, z + z_step(j, up) * (1 - core), core)

    def back(p, j):
        return lax.rem(p + SIDE - j, SIDE)

    def remote(src, dst, ssem, rsem, dev):
        return pltpu.make_async_remote_copy(
            src_ref=src, dst_ref=dst, send_sem=ssem, recv_sem=rsem, device_id=dev,
            device_id_type=MESH,
        )

    own_rows = pl.ds(pl.multiple_of(core * HALF_ROWS, HALF_ROWS), HALF_ROWS)
    other_rows = pl.ds(pl.multiple_of((1 - core) * HALF_ROWS, HALF_ROWS), HALF_ROWS)
    own_points = pl.ds(pl.multiple_of(y * 2 * PIECE + core * PIECE, PIECE), PIECE)
    load_val = pltpu.make_async_copy(valence_ref, val.at[core], loc_sem.at[0])
    load_scr = pltpu.make_async_copy(screened_ref.at[own_rows, :], scr.at[core], loc_sem.at[1])
    load_gath = pltpu.make_async_copy(
        conduction_ref.at[:, own_points], gath.at[core, pb, pa], loc_sem.at[2]
    )
    load_left = pltpu.make_async_copy(conduction_ref, left, loc_sem.at[3])
    for load in (load_val, load_scr, load_gath, load_left):
        load.start()

    peers = [sibling, opposite]
    peers += [y_peer(j) for j in (1, 2, 3)]
    peers += [device(x + j, y, z, core) for j in (1, 2, 3)]
    peers += [device(x, y, z + j, core) for j in (1, -1, 2, -2)]
    barrier = pltpu.get_barrier_semaphore()
    for peer in peers:
        pl.semaphore_signal(barrier, inc=1, device_id=peer, device_id_type=MESH)
    pl.semaphore_wait(barrier, len(peers))

    give_val = remote(valence_ref, val.at[core], pair_send.at[0], pair_recv.at[0], sibling)
    give_scr = remote(
        screened_ref.at[other_rows, :], scr.at[core], pair_send.at[1], pair_recv.at[1], sibling
    )
    give_val.start()
    give_scr.start()

    def gather(buf, own, send_a, recv_a, send_b, recv_b, send_s, recv_s):
        low, high = pl.ds(0, 2), pl.ds(2, 2)

        def step_a(j):
            return remote(
                own, buf.at[core, pb, pa], send_a.at[j - 1], recv_a.at[j - 1], peer_a(j)
            )

        def got_a(j):
            place = buf.at[core, pb, back(pa, j)]
            return remote(place, place, send_a.at[j - 1], recv_a.at[j - 1], peer_a(j))

        def step_b(i):
            if i < 2:
                place = buf.at[core, pb]
                return remote(place, place, send_b.at[i], recv_b.at[i], peer_b((1, 3)[i], 0))
            place = buf.at[core, pb, (low, high)[i - 2]]
            return remote(place, place, send_b.at[i], recv_b.at[i], peer_b(2, i - 2))

        def got_b(i):
            if i < 2:
                place = buf.at[core, back(pb, (1, 3)[i])]
            else:
                place = buf.at[core, back(pb, 2), (low, high)[i - 2]]
            return remote(place, place, send_b.at[i], recv_b.at[i], sibling)

        def step_s(i):
            place = buf.at[core, back(pb, (0, 1, 3, 2)[i])]
            return remote(place, place, send_s.at[i], recv_s.at[i], sibling)

        def got_s(i):
            place = buf.at[1 - core, i]
            return remote(place, place, send_s.at[i], recv_s.at[i], sibling)

        def start_a():
            for j in (1, 3, 2):
                step_a(j).start()

        def a_to_b():
            for j in (1, 3, 2):
                got_a(j).wait_recv()
            for i in range(4):
                step_b(i).start()
            step_s(0).start()

        def b_to_s():
            for i in range(2):
                got_b(i).wait_recv()
                step_s(i + 1).start()
            for i in range(2, 4):
                got_b(i).wait_recv()
            step_s(3).start()

        def finish_s():
            for i in range(4):
                got_s(i).wait_recv()

        def drain():
            for j in (1, 2, 3):
                step_a(j).wait_send()
            for i in range(4):
                step_b(i).wait_send()
                step_s(i).wait_send()

        return start_a, a_to_b, b_to_s, finish_s, drain

    cond_a, cond_ab, cond_bs, cond_s, cond_drain = gather(
        gath, conduction_ref.at[:, own_points], ga_send, ga_recv, gb_send, gb_recv, gs_send, gs_recv
    )
    cond_a()

    band = lax.broadcasted_iota(jnp.int32, (val.shape[2], PAIRS), 0)
    first_pick = jnp.where(band == first_ref[...], 1.0, 0.0).astype(BF16)
    second_pick = jnp.where(band == second_ref[...], 1.0, 0.0).astype(BF16)

    def densities(which):
        for part in range(2):
            rows = pl.ds(part * 256, 256)
            points = val[which, rows, :]
            first_cols = jnp.dot(points, first_pick, preferred_element_type=F32)
            second_cols = jnp.dot(points, second_pick, preferred_element_type=F32)
            dens[which, rows, :] = (first_cols * second_cols).astype(BF16)

    load_val.wait()
    densities(core)
    give_val.wait_recv()
    densities(1 - core)

    load_gath.wait()
    cond_ab()

    load_scr.wait()
    give_scr.wait_recv()
    for v in range(SIDE):
        cols = pl.ds(v * OWN_PAIRS, OWN_PAIRS)
        total = jnp.dot(scr[0], dens[0, :, cols], preferred_element_type=F32)
        total += jnp.dot(scr[1], dens[1, :, cols], preferred_element_type=F32)
        sums[v] = total
        tosend[v] = total.astype(BF16)

    def y_step(j):
        return remote(
            tosend.at[lax.rem(y + j, SIDE)], parts.at[j - 1], y_send.at[j - 1], y_recv.at[j - 1],
            y_peer(j),
        )

    for j in (1, 3, 2):
        y_step(j).start()
    for j in (1, 3, 2):
        y_step(j).wait_recv()
    summed = sums[y]
    for j in (1, 2, 3):
        summed += parts[j - 1].astype(F32)
    zout[...] = summed.astype(BF16)
    sums[0] = summed
    z_copy = remote(zout, zin, z_send, z_recv, opposite)
    z_copy.start()

    cond_bs()
    cond_s()
    for s in range(SLOTS):
        block = jnp.maximum(partners_ref[s], 0)
        block_z = block // SIDE
        block_x = lax.rem(block, SIDE)
        rows = pl.ds(s * BANDS, BANDS)
        sel[y, 0, rows, :] = gath[0, block_z, block_x]
        sel[y, 1, rows, :] = gath[1, block_x, block_z]

    def sel_step(j, h):
        place = sel.at[y, h]
        return remote(place, place, sel_send.at[j - 1, h], sel_recv.at[j - 1, h], y_peer(j))

    for h in range(2):
        for j in (1, 3):
            sel_step(j, h).start()
    for h in range(2):
        sel_step(2, h).start()

    z_copy.wait_recv()
    mix[core, pb, pa] = (sums[0] + zin[...].astype(F32)).astype(BF16)
    mix_a, mix_ab, mix_bs, mix_s, mix_drain = gather(
        mix, mix.at[core, pb, pa], ma_send, ma_recv, mb_send, mb_recv, ms_send, ms_recv
    )
    mix_a()
    out_ref[...] = jnp.zeros_like(out_ref)
    load_left.wait()
    mix_ab()
    mix_bs()
    mix_s()

    def unit(u, carry):
        step = u // 2
        half = lax.rem(u, 2)
        ahead = step + step // 2 - 2 * (step // 3)
        q = lax.rem(y + ahead, SIDE)

        @pl.when(step > 0)
        def _():
            sender = lax.rem(SIDE - ahead, SIDE)
            place = sel.at[q, half]
            remote(
                place, place, sel_send.at[sender - 1, half], sel_recv.at[sender - 1, half], sibling
            ).wait_recv()

        mixed = jnp.concatenate(
            [
                mix[0, q, 2 * half],
                mix[1, 2 * half, q],
                mix[0, q, 2 * half + 1],
                mix[1, 2 * half + 1, q],
            ],
            0,
        )
        points = pl.ds(pl.multiple_of(q * 2 * PIECE + half * PIECE, PIECE), PIECE)
        for s in range(SLOTS):
            right = sel[q, half, s * BANDS : (s + 1) * BANDS, :]
            rows = [
                jnp.broadcast_to(left[i : i + 1, points], right.shape) * right
                for i in range(BANDS)
            ]
            density = jnp.concatenate(rows, 0)
            out_ref[s] += jnp.dot(density, mixed, preferred_element_type=F32)
        return carry

    lax.fori_loop(0, 2 * SIDE, unit, 0)
    for s in range(SLOTS):
        scale = jnp.where(partners_ref[s] >= 0, 1.0 / math.sqrt(POINTS), 0.0)
        out_ref[s] = out_ref[s] * scale

    give_val.wait_send()
    give_scr.wait_send()
    for j in (1, 2, 3):
        y_step(j).wait_send()
        for h in range(2):
            sel_step(j, h).wait_send()
    z_copy.wait_send()
    cond_drain()
    mix_drain()


def on_device(screened, valence, first_band, second_band, conduction, partners):
    vmem = pl.BlockSpec(memory_space=pltpu.VMEM)
    hbm = pl.BlockSpec(memory_space=pl.ANY)
    dma = pltpu.SemaphoreType.DMA
    kernel = pl.pallas_call(
        whole_kernel,
        out_shape=jax.ShapeDtypeStruct((SLOTS, BANDS * BANDS, OWN_PAIRS), F32),
        in_specs=[pl.BlockSpec(memory_space=pltpu.SMEM), vmem, vmem, hbm, hbm, hbm],
        out_specs=vmem,
        scratch_shapes=[
            pltpu.VMEM((BANDS, POINTS), BF16),
            pltpu.VMEM((2, HALF_ROWS, 512), BF16),
            pltpu.VMEM((2, 512, 256), BF16),
            pltpu.VMEM((2, 512, PAIRS), BF16),
            pltpu.VMEM((SIDE, HALF_ROWS, OWN_PAIRS), F32),
            pltpu.VMEM((SIDE, HALF_ROWS, OWN_PAIRS), BF16),
            pltpu.VMEM((SIDE - 1, HALF_ROWS, OWN_PAIRS), BF16),
            pltpu.VMEM((HALF_ROWS, OWN_PAIRS), BF16),
            pltpu.VMEM((HALF_ROWS, OWN_PAIRS), BF16),
            pltpu.VMEM((2, SIDE, SIDE, BANDS, PIECE), BF16),
            pltpu.VMEM((2, SIDE, SIDE, HALF_ROWS, OWN_PAIRS), BF16),
            pltpu.VMEM((SIDE, 2, SLOTS * BANDS, PIECE), BF16),
            dma((4,)),
            dma((2,)),
            dma((2,)),
            dma((3,)),
            dma((3,)),
            dma,
            dma,
        ]
        + [dma((3,)), dma((3,)), dma((4,)), dma((4,)), dma((4,)), dma((4,))] * 2
        + [dma((3, 2)), dma((3, 2))],
        compiler_params=pltpu.CompilerParams(
            collective_id=0, has_side_effects=True, vmem_limit_bytes=48 * 2**20
        ),
    )(
        partners.reshape(-1),
        first_band.reshape(1, -1),
        second_band.reshape(1, -1),
        screened,
        valence,
        conduction,
    )
    return kernel.reshape((1, 1) + kernel.shape)


def solution(mesh):
    in_specs = (
        P("cond", ("grp", "val")),
        P(("grp", "val"), None),
        P(),
        P(),
        P("cond", None),
        P("grp", "cond", None),
    )
    out_specs = P("grp", "cond", None, None, "val")
    return jax.shard_map(
        on_device, mesh=mesh, in_specs=in_specs, out_specs=out_specs, check_vma=False
    )
```

```python
import math

import jax
import jax.numpy as jnp
from jax import lax
from jax.experimental import pallas as pl
from jax.experimental.pallas import tpu as pltpu
from jax.sharding import PartitionSpec as P

MESH = pl.DeviceIdType.MESH
BF16 = jnp.bfloat16
F32 = jnp.float32
SIDE = 4
BANDS = 32
SLOTS = 4
POINTS = 8192
PAIRS = 512
OWN_PAIRS = 128
HALF_ROWS = 256
CHUNKS = 2
STRIP = HALF_ROWS // CHUNKS
QUARTER = POINTS // SIDE
PART = SIDE * STRIP


def whole_kernel(
    partners_ref,
    first_ref,
    second_ref,
    screened_ref,
    valence_ref,
    conduction_ref,
    out_ref,
    partners,
    bands,
    natural,
    left,
    scr,
    val,
    dens,
    pair_out,
    pair_in,
    sums,
    tosend,
    parts,
    zout,
    zin,
    gath_first,
    gath_second,
    mix,
    sel,
    sib,
    load_sem,
    pair_send,
    pair_recv,
    y_send,
    y_recv,
    z_send,
    z_recv,
    ga_send,
    ga_recv,
    gb_send,
    gb_recv,
    ma_send,
    ma_recv,
    mb_send,
    mb_recv,
    ms_send,
    ms_recv,
    own_send,
    other_send,
    near_recv,
    sib_send,
    sib_recv,
    relay_send,
    relay_recv,
):
    grp = lax.axis_index("grp")
    cond = lax.axis_index("cond")
    y = lax.axis_index("val")
    core = lax.rem(grp, 2)
    x = lax.rem(cond, SIDE)
    zlo = cond // SIDE
    z = (grp // 2) * SIDE + zlo
    par = lax.rem(x, 2)

    def device(px, py, pz, pcore):
        px = lax.rem(px + SIDE, SIDE)
        py = lax.rem(py + SIDE, SIDE)
        pz = lax.rem(pz + 2 * SIDE, 2 * SIDE)
        return ((pz // SIDE) * 2 + pcore, lax.rem(pz, SIDE) * SIDE + px, py)

    sibling = device(x, y, z, 1 - core)
    opposite = device(x, y, z + SIDE, core)

    def z_step(j, up):
        return (0, 1, up * 4 - 2, -1)[j]

    pa = x * (1 - core) + zlo * core
    pb = zlo * (1 - core) + x * core

    def peer_a(j):
        return device(x + j * (1 - core), y, z + z_step(j, par) * core, core)

    def peer_b(j, up):
        return device(x + j * core, y, z + z_step(j, up) * (1 - core), core)

    def back(p, j):
        return lax.rem(p + SIDE - j, SIDE)

    def remote(src, dst, ssem, rsem, dev):
        return pltpu.make_async_remote_copy(
            src_ref=src, dst_ref=dst, send_sem=ssem, recv_sem=rsem, device_id=dev,
            device_id_type=MESH,
        )

    copies = [
        (conduction_ref, natural),
        (first_ref, bands.at[0]),
        (second_ref, bands.at[1]),
        (valence_ref, val),
        (screened_ref, scr),
        (partners_ref, partners.at[0]),
    ]
    loads = [
        pltpu.make_async_copy(src, dst, load_sem.at[i]) for i, (src, dst) in enumerate(copies)
    ]
    load_natural, load_first, load_second, load_val, load_scr, load_partners = loads
    for load in loads:
        load.start()

    peers = [sibling, opposite]
    peers += [device(x, y + j, z, core) for j in (1, 2, 3)]
    peers += [device(x, y + j, z, 1 - core) for j in (1, 3)]
    peers += [device(x + j, y, z, core) for j in (1, 2, 3)]
    peers += [device(x, y, z + j, core) for j in (1, -1, 2, -2)]
    barrier = pltpu.get_barrier_semaphore()
    for peer in peers:
        pl.semaphore_signal(barrier, inc=1, device_id=peer, device_id_type=MESH)

    load_natural.wait()
    for q in range(SIDE):
        for t in range(CHUNKS):
            for h in range(2):
                for i in range(SIDE):
                    start = q * QUARTER + i * 2 * HALF_ROWS + h * HALF_ROWS + t * STRIP
                    left[q, t, h, :, i * STRIP : (i + 1) * STRIP] = natural[
                        :, start : start + STRIP
                    ]

    load_first.wait()
    load_second.wait()
    band = lax.broadcasted_iota(jnp.int32, (val.shape[1], PAIRS), 0)
    first_pick = jnp.where(band == bands[0], 1.0, 0.0).astype(BF16)
    second_pick = jnp.where(band == bands[1], 1.0, 0.0).astype(BF16)
    load_val.wait()
    for part in range(2):
        rows = pl.ds(part * 256, 256)
        points = val[rows, :]
        first_cols = jnp.dot(points, first_pick, preferred_element_type=F32)
        second_cols = jnp.dot(points, second_pick, preferred_element_type=F32)
        dens[rows, :] = (first_cols * second_cols).astype(BF16)
    load_scr.wait()
    for owner, kept in ((1 - core, pair_out), (core, sums)):
        for t in range(CHUNKS):
            start = pl.multiple_of(owner * HALF_ROWS + t * STRIP, STRIP)
            total = jnp.dot(scr[pl.ds(start, STRIP), :], dens[...], preferred_element_type=F32)
            for v in range(SIDE):
                kept[t, v] = total[:, v * OWN_PAIRS : (v + 1) * OWN_PAIRS]

    pl.semaphore_wait(barrier, len(peers))

    def pair_step(t):
        return remote(pair_out.at[t], pair_in.at[t], pair_send.at[t], pair_recv.at[t], sibling)

    give_partners = remote(
        partners_ref, partners.at[1], pair_send.at[CHUNKS], pair_recv.at[CHUNKS], sibling
    )
    for t in range(CHUNKS):
        pair_step(t).start()
    give_partners.start()

    low, high = pl.ds(0, 2), pl.ds(2, 2)

    class Gather:
        def __init__(self, buf, own, t, send_a, recv_a, send_b, recv_b):
            self.buf, self.own, self.t = buf, own, t
            self.send_a, self.recv_a, self.send_b, self.recv_b = send_a, recv_a, send_b, recv_b

        def step_a(self, j):
            sems = self.send_a.at[self.t, j - 1], self.recv_a.at[self.t, j - 1]
            return remote(self.own, self.buf.at[pb, pa], *sems, peer_a(j))

        def got_a(self, j):
            place = self.buf.at[pb, back(pa, j)]
            sems = self.send_a.at[self.t, j - 1], self.recv_a.at[self.t, j - 1]
            return remote(place, place, *sems, peer_a(j))

        def step_b(self, i):
            sems = self.send_b.at[self.t, i], self.recv_b.at[self.t, i]
            if i < 2:
                place = self.buf.at[pb]
                return remote(place, place, *sems, peer_b((1, 3)[i], 0))
            place = self.buf.at[pb, (low, high)[i - 2]]
            return remote(place, place, *sems, peer_b(2, i - 2))

        def got_b(self, i):
            sems = self.send_b.at[self.t, i], self.recv_b.at[self.t, i]
            if i < 2:
                place = self.buf.at[back(pb, (1, 3)[i])]
            else:
                place = self.buf.at[back(pb, 2), (low, high)[i - 2]]
            return remote(place, place, *sems, sibling)

        def start_a(self):
            for j in (1, 3, 2):
                self.step_a(j).start()

        def a_to_b(self):
            for j in (1, 3, 2):
                self.got_a(j).wait_recv()
            for i in range(4):
                self.step_b(i).start()

        def drain(self):
            for j in (1, 2, 3):
                self.step_a(j).wait_send()
            for i in range(4):
                self.step_b(i).wait_send()

    gath = (gath_first, gath_second)
    cond_gather = [
        Gather(gath[t], left.at[y, t, core], t, ga_send, ga_recv, gb_send, gb_recv)
        for t in range(CHUNKS)
    ]
    for t in range(CHUNKS):
        cond_gather[t].start_a()
        gath[t][pb, pa] = left[y, t, core]

    def y_step(j, t):
        return remote(
            tosend.at[t, lax.rem(y + j, SIDE)], parts.at[t, j - 1], y_send.at[t, j - 1],
            y_recv.at[t, j - 1], device(x, y + j, z, core),
        )

    for t in range(CHUNKS):
        pair_step(t).wait_recv()
        for v in range(SIDE):
            block = sums[t, v] + pair_in[t, v]
            sums[t, v] = block
            tosend[t, v] = block.astype(BF16)
        for j in (1, 3, 2):
            y_step(j, t).start()

    def z_copy(t):
        return remote(zout.at[t], zin.at[t], z_send.at[t], z_recv.at[t], opposite)

    for t in range(CHUNKS):
        for j in (1, 3, 2):
            y_step(j, t).wait_recv()
        summed = sums[t, y]
        for j in (1, 2, 3):
            summed += parts[t, j - 1].astype(F32)
        zout[t] = summed.astype(BF16)
        sums[t, 0] = summed
        z_copy(t).start()
    for t in range(CHUNKS):
        cond_gather[t].a_to_b()

    def own_step(j, t):
        place = sel.at[y, core, t]
        i = (j - 1) // 2
        return remote(
            place, place, own_send.at[t, i], near_recv.at[t, i, core], device(x, y + j, z, core)
        )

    def other_step(j, t):
        i = (j - 1) // 2
        return remote(
            sib.at[t], sel.at[y, core, t], other_send.at[t, i], near_recv.at[t, i, core],
            device(x, y + j, z, 1 - core),
        )

    def sib_step(t):
        return remote(sib.at[t], sel.at[y, core, t], sib_send.at[t], sib_recv.at[t], sibling)

    def near_got(j, h, t):
        place = sel.at[back(y, j), h, t]
        i = (j - 1) // 2
        return remote(place, place, own_send.at[t, i], near_recv.at[t, i, h], sibling)

    def relay_step(h, t):
        place = sel.at[back(y, (1, 3)[h]), h, t]
        return remote(
            place, place, relay_send.at[t, h], relay_recv.at[t, h],
            device(x, y + (1, 3)[h], z, core),
        )

    def relay(t):
        near_got(1, 0, t).wait_recv()
        relay_step(0, t).start()
        near_got(3, 1, t).wait_recv()
        relay_step(1, t).start()

    mix_gather = [
        Gather(mix.at[core, t], mix.at[core, t, pb, pa], t, ma_send, ma_recv, mb_send, mb_recv)
        for t in range(CHUNKS)
    ]

    def cross_step(i, t):
        place = mix.at[core, t, back(pb, (0, 1, 3, 2)[i])]
        return remote(place, place, ms_send.at[t, i], ms_recv.at[t, i], sibling)

    def cross_got(i, t):
        place = mix.at[1 - core, t, i]
        return remote(place, place, ms_send.at[t, i], ms_recv.at[t, i], sibling)

    def b_to_cross(t):
        for i in range(2):
            mix_gather[t].got_b(i).wait_recv()
            cross_step(i + 1, t).start()
        for i in range(2, 4):
            mix_gather[t].got_b(i).wait_recv()
        cross_step(3, t).start()

    def cross_all(t):
        for i in range(4):
            cross_got(i, t).wait_recv()

    for t in range(CHUNKS):
        z_copy(t).wait_recv()
        mix[core, t, pb, pa] = (sums[t, 0] + zin[t].astype(F32)).astype(BF16)
        mix_gather[t].start_a()
    load_partners.wait()
    give_partners.wait_recv()
    for t in range(CHUNKS):
        for i in range(4):
            cond_gather[t].got_b(i).wait_recv()
        for s in range(SLOTS):
            rows = pl.ds(s * BANDS, BANDS)
            for which in range(2):
                block = jnp.maximum(partners[which, s], 0)
                block_z = block // SIDE
                block_x = lax.rem(block, SIDE)
                picked = gath[t][
                    block_z * (1 - core) + block_x * core,
                    block_x * (1 - core) + block_z * core,
                ]
                if which == 0:
                    sel[y, core, t, rows, :] = picked
                else:
                    sib[t, rows, :] = picked
        for j in (1, 3):
            own_step(j, t).start()
            other_step(j, t).start()
        sib_step(t).start()

    out_ref[...] = jnp.zeros_like(out_ref)
    for t in range(CHUNKS):
        mix_gather[t].a_to_b()
        cross_step(0, t).start()
    relay(0)
    b_to_cross(0)
    cross_all(0)

    def unit(u, carry):
        t = u // SIDE
        step = lax.rem(u, SIDE)
        ahead = step + step // 2 - 2 * (step // 3)
        q = lax.rem(y + ahead, SIDE)

        def arrived(h, sem):
            place = sel.at[q, h, t]
            remote(place, place, own_send.at[0, 0], sem, sibling).wait_recv()

        @pl.when(step == 0)
        def _():
            arrived(1 - core, sib_recv.at[t])

        @pl.when(step == 1)
        def _():
            arrived(0, near_recv.at[t, 1, 0])

        @pl.when(step == 2)
        def _():
            arrived(1, near_recv.at[t, 0, 1])

        @pl.when(step == 3)
        def _():
            arrived(0, relay_recv.at[t, 0])
            arrived(1, relay_recv.at[t, 1])

        @pl.when(u == 1)
        def _():
            b_to_cross(1)

        @pl.when(u == 2)
        def _():
            relay(1)

        @pl.when(u == SIDE)
        def _():
            cross_all(1)

        mixed = jnp.concatenate(
            [mix[0, t, q, i] for i in range(SIDE)] + [mix[1, t, i, q] for i in range(SIDE)], 0
        )
        for s in range(SLOTS):
            rows = slice(s * BANDS, (s + 1) * BANDS)
            right = jnp.concatenate([sel[q, 0, t, rows, :], sel[q, 1, t, rows, :]], 1)
            blocks = []
            for i in range(BANDS):
                row = jnp.concatenate(
                    [left[q, t, 0, i : i + 1, :], left[q, t, 1, i : i + 1, :]], 1
                )
                blocks.append(jnp.broadcast_to(row, right.shape) * right)
            density = jnp.concatenate(blocks, 0)
            out_ref[s] += jnp.dot(density, mixed, preferred_element_type=F32)
        return carry

    lax.fori_loop(0, CHUNKS * SIDE, unit, 0)
    for s in range(SLOTS):
        scale = jnp.where(partners[0, s] >= 0, 1.0 / math.sqrt(POINTS), 0.0)
        out_ref[s] = out_ref[s] * scale

    give_partners.wait_send()
    for t in range(CHUNKS):
        pair_step(t).wait_send()
        for j in (1, 2, 3):
            y_step(j, t).wait_send()
        z_copy(t).wait_send()
        for j in (1, 3):
            own_step(j, t).wait_send()
            other_step(j, t).wait_send()
        sib_step(t).wait_send()
        for h in range(2):
            relay_step(h, t).wait_send()
        for i in range(4):
            cross_step(i, t).wait_send()
        cond_gather[t].drain()
        mix_gather[t].drain()


def on_device(screened, valence, first_band, second_band, conduction, partners):
    vmem = pl.BlockSpec(memory_space=pltpu.VMEM)
    hbm = pl.BlockSpec(memory_space=pltpu.HBM)
    dma = pltpu.SemaphoreType.DMA
    kernel = pl.pallas_call(
        whole_kernel,
        out_shape=jax.ShapeDtypeStruct((SLOTS, BANDS * BANDS, OWN_PAIRS), F32),
        in_specs=[hbm] * 6,
        out_specs=vmem,
        scratch_shapes=[
            pltpu.SMEM((2, SLOTS), jnp.int32),
            pltpu.VMEM((2, 1, PAIRS), jnp.int32),
            pltpu.VMEM((BANDS, POINTS), BF16),
            pltpu.VMEM((SIDE, CHUNKS, 2, BANDS, PART), BF16),
            pltpu.VMEM((2 * HALF_ROWS, 512), BF16),
            pltpu.VMEM((512, 256), BF16),
            pltpu.VMEM((512, PAIRS), BF16),
            pltpu.VMEM((CHUNKS, SIDE, STRIP, OWN_PAIRS), F32),
            pltpu.VMEM((CHUNKS, SIDE, STRIP, OWN_PAIRS), F32),
            pltpu.VMEM((CHUNKS, SIDE, STRIP, OWN_PAIRS), F32),
            pltpu.VMEM((CHUNKS, SIDE, STRIP, OWN_PAIRS), BF16),
            pltpu.VMEM((CHUNKS, SIDE - 1, STRIP, OWN_PAIRS), BF16),
            pltpu.VMEM((CHUNKS, STRIP, OWN_PAIRS), BF16),
            pltpu.VMEM((CHUNKS, STRIP, OWN_PAIRS), BF16),
            pltpu.VMEM((SIDE, SIDE, BANDS, PART), BF16),
            pltpu.VMEM((SIDE, SIDE, BANDS, PART), BF16),
            pltpu.VMEM((2, CHUNKS, SIDE, SIDE, STRIP, OWN_PAIRS), BF16),
            pltpu.VMEM((SIDE, 2, CHUNKS, SLOTS * BANDS, PART), BF16),
            pltpu.VMEM((CHUNKS, SLOTS * BANDS, PART), BF16),
            dma((6,)),
            dma((3,)),
            dma((3,)),
            dma((CHUNKS, 3)),
            dma((CHUNKS, 3)),
            dma((CHUNKS,)),
            dma((CHUNKS,)),
        ]
        + [dma((CHUNKS, 3)), dma((CHUNKS, 3)), dma((CHUNKS, 4)), dma((CHUNKS, 4))] * 2
        + [
            dma((CHUNKS, 4)),
            dma((CHUNKS, 4)),
            dma((CHUNKS, 2)),
            dma((CHUNKS, 2)),
            dma((CHUNKS, 2, 2)),
            dma((CHUNKS,)),
            dma((CHUNKS,)),
            dma((CHUNKS, 2)),
            dma((CHUNKS, 2)),
        ],
        compiler_params=pltpu.CompilerParams(
            collective_id=0, has_side_effects=True, vmem_limit_bytes=63 * 2**20
        ),
    )(
        partners.reshape(-1),
        first_band.reshape(1, -1),
        second_band.reshape(1, -1),
        screened,
        valence,
        conduction,
    )
    return kernel.reshape((1, 1) + kernel.shape)


def solution(mesh):
    in_specs = (
        P("cond", ("grp", "val")),
        P(("grp", "val"), None),
        P(),
        P(),
        P("cond", None),
        P("grp", "cond", None),
    )
    out_specs = P("grp", "cond", None, None, "val")
    return jax.shard_map(
        on_device, mesh=mesh, in_specs=in_specs, out_specs=out_specs, check_vma=False
    )
```

```python
import math

import jax
import jax.numpy as jnp
from jax import lax
from jax.experimental import pallas as pl
from jax.experimental.pallas import tpu as pltpu
from jax.sharding import PartitionSpec as P

MESH = pl.DeviceIdType.MESH
BF16 = jnp.bfloat16
F32 = jnp.float32
SIDE = 4
BANDS = 32
SLOTS = 4
POINTS = 8192
PAIRS = 512
OWN_PAIRS = 128
HALF_ROWS = 256
CHUNKS = 2
STRIP = HALF_ROWS // CHUNKS
QUARTER = POINTS // SIDE
PART = SIDE * STRIP


def whole_kernel(
    partners_ref,
    first_ref,
    second_ref,
    screened_ref,
    valence_ref,
    conduction_ref,
    final_ref,
    out_ref,
    out_sem,
    partners,
    bands,
    natural,
    left,
    scr,
    val,
    dens,
    pair_out,
    pair_in,
    sums,
    tosend,
    parts,
    zout,
    zin,
    gath_first,
    gath_second,
    mix,
    sel,
    sib,
    load_sem,
    pair_send,
    pair_recv,
    y_send,
    y_recv,
    z_send,
    z_recv,
    ga_send,
    ga_recv,
    gb_send,
    gb_recv,
    ma_send,
    ma_recv,
    mb_send,
    mb_recv,
    ms_send,
    ms_recv,
    own_send,
    other_send,
    near_recv,
    sib_send,
    sib_recv,
    relay_send,
    relay_recv,
):
    grp = lax.axis_index("grp")
    cond = lax.axis_index("cond")
    y = lax.axis_index("val")
    core = lax.rem(grp, 2)
    x = lax.rem(cond, SIDE)
    zlo = cond // SIDE
    z = (grp // 2) * SIDE + zlo
    par = lax.rem(x, 2)

    def device(px, py, pz, pcore):
        px = lax.rem(px + SIDE, SIDE)
        py = lax.rem(py + SIDE, SIDE)
        pz = lax.rem(pz + 2 * SIDE, 2 * SIDE)
        return ((pz // SIDE) * 2 + pcore, lax.rem(pz, SIDE) * SIDE + px, py)

    sibling = device(x, y, z, 1 - core)
    opposite = device(x, y, z + SIDE, core)

    def z_step(j, up):
        return (0, 1, up * 4 - 2, -1)[j]

    pa = x * (1 - core) + zlo * core
    pb = zlo * (1 - core) + x * core

    def peer_a(j):
        return device(x + j * (1 - core), y, z + z_step(j, par) * core, core)

    def peer_b(j, up):
        return device(x + j * core, y, z + z_step(j, up) * (1 - core), core)

    def back(p, j):
        return lax.rem(p + SIDE - j, SIDE)

    def remote(src, dst, ssem, rsem, dev):
        return pltpu.make_async_remote_copy(
            src_ref=src, dst_ref=dst, send_sem=ssem, recv_sem=rsem, device_id=dev,
            device_id_type=MESH,
        )

    copies = [
        (conduction_ref, natural),
        (first_ref, bands.at[0]),
        (second_ref, bands.at[1]),
        (valence_ref, val),
        (screened_ref, scr),
        (partners_ref, partners.at[0]),
    ]
    loads = [
        pltpu.make_async_copy(src, dst, load_sem.at[i]) for i, (src, dst) in enumerate(copies)
    ]
    load_natural, load_first, load_second, load_val, load_scr, load_partners = loads
    for load in loads:
        load.start()

    peers = [sibling, opposite]
    peers += [device(x, y + j, z, core) for j in (1, 2, 3)]
    peers += [device(x, y + j, z, 1 - core) for j in (1, 3)]
    peers += [device(x + j, y, z, core) for j in (1, 2, 3)]
    peers += [device(x, y, z + j, core) for j in (1, -1, 2, -2)]
    barrier = pltpu.get_barrier_semaphore()
    for peer in peers:
        pl.semaphore_signal(barrier, inc=1, device_id=peer, device_id_type=MESH)

    load_natural.wait()
    for q in range(SIDE):
        for t in range(CHUNKS):
            for h in range(2):
                for i in range(SIDE):
                    start = q * QUARTER + i * 2 * HALF_ROWS + h * HALF_ROWS + t * STRIP
                    left[q, t, h, :, i * STRIP : (i + 1) * STRIP] = natural[
                        :, start : start + STRIP
                    ]

    load_first.wait()
    load_second.wait()
    band = lax.broadcasted_iota(jnp.int32, (val.shape[1], PAIRS), 0)
    first_pick = jnp.where(band == bands[0], 1.0, 0.0).astype(BF16)
    second_pick = jnp.where(band == bands[1], 1.0, 0.0).astype(BF16)
    load_val.wait()
    for part in range(2):
        rows = pl.ds(part * 256, 256)
        points = val[rows, :]
        first_cols = jnp.dot(points, first_pick, preferred_element_type=F32)
        second_cols = jnp.dot(points, second_pick, preferred_element_type=F32)
        dens[rows, :] = (first_cols * second_cols).astype(BF16)
    load_scr.wait()
    for owner, kept in ((1 - core, pair_out), (core, sums)):
        for t in range(CHUNKS):
            start = pl.multiple_of(owner * HALF_ROWS + t * STRIP, STRIP)
            total = jnp.dot(scr[pl.ds(start, STRIP), :], dens[...], preferred_element_type=F32)
            for v in range(SIDE):
                kept[t, v] = total[:, v * OWN_PAIRS : (v + 1) * OWN_PAIRS]

    pl.semaphore_wait(barrier, len(peers))

    def pair_step(t):
        return remote(pair_out.at[t], pair_in.at[t], pair_send.at[t], pair_recv.at[t], sibling)

    give_partners = remote(
        partners_ref, partners.at[1], pair_send.at[CHUNKS], pair_recv.at[CHUNKS], sibling
    )
    for t in range(CHUNKS):
        pair_step(t).start()
    give_partners.start()

    low, high = pl.ds(0, 2), pl.ds(2, 2)

    class Gather:
        def __init__(self, buf, own, t, send_a, recv_a, send_b, recv_b):
            self.buf, self.own, self.t = buf, own, t
            self.send_a, self.recv_a, self.send_b, self.recv_b = send_a, recv_a, send_b, recv_b

        def step_a(self, j):
            sems = self.send_a.at[self.t, j - 1], self.recv_a.at[self.t, j - 1]
            return remote(self.own, self.buf.at[pb, pa], *sems, peer_a(j))

        def got_a(self, j):
            place = self.buf.at[pb, back(pa, j)]
            sems = self.send_a.at[self.t, j - 1], self.recv_a.at[self.t, j - 1]
            return remote(place, place, *sems, peer_a(j))

        def step_b(self, i):
            sems = self.send_b.at[self.t, i], self.recv_b.at[self.t, i]
            if i < 2:
                place = self.buf.at[pb]
                return remote(place, place, *sems, peer_b((1, 3)[i], 0))
            place = self.buf.at[pb, (low, high)[i - 2]]
            return remote(place, place, *sems, peer_b(2, i - 2))

        def got_b(self, i):
            sems = self.send_b.at[self.t, i], self.recv_b.at[self.t, i]
            if i < 2:
                place = self.buf.at[back(pb, (1, 3)[i])]
            else:
                place = self.buf.at[back(pb, 2), (low, high)[i - 2]]
            return remote(place, place, *sems, sibling)

        def start_a(self):
            for j in (1, 3, 2):
                self.step_a(j).start()

        def a_to_b(self):
            for j in (1, 3, 2):
                self.got_a(j).wait_recv()
            for i in range(4):
                self.step_b(i).start()

        def drain(self):
            for j in (1, 2, 3):
                self.step_a(j).wait_send()
            for i in range(4):
                self.step_b(i).wait_send()

    gath = (gath_first, gath_second)
    cond_gather = [
        Gather(gath[t], left.at[y, t, core], t, ga_send, ga_recv, gb_send, gb_recv)
        for t in range(CHUNKS)
    ]
    for t in range(CHUNKS):
        cond_gather[t].start_a()
        gath[t][pb, pa] = left[y, t, core]

    def y_step(j, t):
        return remote(
            tosend.at[t, lax.rem(y + j, SIDE)], parts.at[t, j - 1], y_send.at[t, j - 1],
            y_recv.at[t, j - 1], device(x, y + j, z, core),
        )

    for t in range(CHUNKS):
        pair_step(t).wait_recv()
        for v in range(SIDE):
            block = sums[t, v] + pair_in[t, v]
            sums[t, v] = block
            tosend[t, v] = block.astype(BF16)
        for j in (1, 3, 2):
            y_step(j, t).start()

    def z_copy(t):
        return remote(zout.at[t], zin.at[t], z_send.at[t], z_recv.at[t], opposite)

    for t in range(CHUNKS):
        for j in (1, 3, 2):
            y_step(j, t).wait_recv()
        summed = sums[t, y]
        for j in (1, 2, 3):
            summed += parts[t, j - 1].astype(F32)
        zout[t] = summed.astype(BF16)
        sums[t, 0] = summed
        z_copy(t).start()
    for t in range(CHUNKS):
        cond_gather[t].a_to_b()

    def own_step(j, t):
        place = sel.at[y, core, t]
        i = (j - 1) // 2
        return remote(
            place, place, own_send.at[t, i], near_recv.at[t, i, core], device(x, y + j, z, core)
        )

    def other_step(j, t):
        i = (j - 1) // 2
        return remote(
            sib.at[t], sel.at[y, core, t], other_send.at[t, i], near_recv.at[t, i, core],
            device(x, y + j, z, 1 - core),
        )

    def sib_step(t):
        return remote(sib.at[t], sel.at[y, core, t], sib_send.at[t], sib_recv.at[t], sibling)

    def near_got(j, h, t):
        place = sel.at[back(y, j), h, t]
        i = (j - 1) // 2
        return remote(place, place, own_send.at[t, i], near_recv.at[t, i, h], sibling)

    def relay_step(h, t):
        place = sel.at[back(y, (1, 3)[h]), h, t]
        return remote(
            place, place, relay_send.at[t, h], relay_recv.at[t, h],
            device(x, y + (1, 3)[h], z, core),
        )

    def relay(t):
        near_got(1, 0, t).wait_recv()
        relay_step(0, t).start()
        near_got(3, 1, t).wait_recv()
        relay_step(1, t).start()

    mix_gather = [
        Gather(mix.at[core, t], mix.at[core, t, pb, pa], t, ma_send, ma_recv, mb_send, mb_recv)
        for t in range(CHUNKS)
    ]

    def cross_step(i, t):
        place = mix.at[core, t, back(pb, (0, 1, 3, 2)[i])]
        return remote(place, place, ms_send.at[t, i], ms_recv.at[t, i], sibling)

    def cross_got(i, t):
        place = mix.at[1 - core, t, i]
        return remote(place, place, ms_send.at[t, i], ms_recv.at[t, i], sibling)

    def b_to_cross(t):
        for i in range(2):
            mix_gather[t].got_b(i).wait_recv()
            cross_step(i + 1, t).start()
        for i in range(2, 4):
            mix_gather[t].got_b(i).wait_recv()
        cross_step(3, t).start()

    def cross_all(t):
        for i in range(4):
            cross_got(i, t).wait_recv()

    for t in range(CHUNKS):
        z_copy(t).wait_recv()
        mix[core, t, pb, pa] = (sums[t, 0] + zin[t].astype(F32)).astype(BF16)
        mix_gather[t].start_a()
    out_ref[...] = jnp.zeros_like(out_ref)
    for t in range(CHUNKS):
        mix_gather[t].a_to_b()
        cross_step(0, t).start()
    load_partners.wait()
    give_partners.wait_recv()
    def pick_and_send(t):
        for i in range(4):
            cond_gather[t].got_b(i).wait_recv()
        for s in range(SLOTS):
            rows = pl.ds(s * BANDS, BANDS)
            for which in range(2):
                block = jnp.maximum(partners[which, s], 0)
                block_z = block // SIDE
                block_x = lax.rem(block, SIDE)
                picked = gath[t][
                    block_z * (1 - core) + block_x * core,
                    block_x * (1 - core) + block_z * core,
                ]
                if which == 0:
                    sel[y, core, t, rows, :] = picked
                else:
                    sib[t, rows, :] = picked
        for j in (1, 3):
            own_step(j, t).start()
            other_step(j, t).start()
        sib_step(t).start()

    pick_and_send(0)
    b_to_cross(0)
    pick_and_send(1)
    cross_all(0)

    def unit(u, carry):
        t = u // SIDE
        step = lax.rem(u, SIDE)
        ahead = step + step // 2 - 2 * (step // 3)
        q = lax.rem(y + ahead, SIDE)

        def arrived(h, sem):
            place = sel.at[q, h, t]
            remote(place, place, own_send.at[0, 0], sem, sibling).wait_recv()

        @pl.when(u == 1)
        def _():
            b_to_cross(1)
            relay(0)

        @pl.when(u == 3)
        def _():
            relay(1)

        @pl.when(step == 0)
        def _():
            arrived(1 - core, sib_recv.at[t])

        @pl.when(step == 1)
        def _():
            arrived(0, near_recv.at[t, 1, 0])

        @pl.when(step == 2)
        def _():
            arrived(1, near_recv.at[t, 0, 1])

        @pl.when(step == 3)
        def _():
            arrived(0, relay_recv.at[t, 0])
            arrived(1, relay_recv.at[t, 1])

        @pl.when(u == SIDE)
        def _():
            cross_all(1)

        mixed = jnp.concatenate(
            [mix[0, t, q, i] for i in range(SIDE)] + [mix[1, t, i, q] for i in range(SIDE)], 0
        )
        for s in range(SLOTS):
            rows = slice(s * BANDS, (s + 1) * BANDS)
            right = jnp.concatenate([sel[q, 0, t, rows, :], sel[q, 1, t, rows, :]], 1)
            blocks = []
            for i in range(BANDS):
                row = jnp.concatenate(
                    [left[q, t, 0, i : i + 1, :], left[q, t, 1, i : i + 1, :]], 1
                )
                blocks.append(jnp.broadcast_to(row, right.shape) * right)
            density = jnp.concatenate(blocks, 0)
            out_ref[s] += jnp.dot(density, mixed, preferred_element_type=F32)
        return carry

    lax.fori_loop(0, CHUNKS * SIDE, unit, 0)
    def write(s):
        return pltpu.make_async_copy(out_ref.at[s], final_ref.at[s], out_sem.at[s])

    for s in range(SLOTS):
        scale = jnp.where(partners[0, s] >= 0, 1.0 / math.sqrt(POINTS), 0.0)
        out_ref[s] = out_ref[s] * scale
        write(s).start()

    give_partners.wait_send()
    for t in range(CHUNKS):
        pair_step(t).wait_send()
        for j in (1, 2, 3):
            y_step(j, t).wait_send()
        z_copy(t).wait_send()
        for j in (1, 3):
            own_step(j, t).wait_send()
            other_step(j, t).wait_send()
        sib_step(t).wait_send()
        for h in range(2):
            relay_step(h, t).wait_send()
        for i in range(4):
            cross_step(i, t).wait_send()
        cond_gather[t].drain()
        mix_gather[t].drain()
    for s in range(SLOTS):
        write(s).wait()


def on_device(screened, valence, first_band, second_band, conduction, partners):
    vmem = pl.BlockSpec(memory_space=pltpu.VMEM)
    hbm = pl.BlockSpec(memory_space=pltpu.HBM)
    dma = pltpu.SemaphoreType.DMA
    kernel = pl.pallas_call(
        whole_kernel,
        out_shape=jax.ShapeDtypeStruct((SLOTS, BANDS * BANDS, OWN_PAIRS), F32),
        in_specs=[hbm] * 6,
        out_specs=hbm,
        scratch_shapes=[
            pltpu.VMEM((SLOTS, BANDS * BANDS, OWN_PAIRS), F32),
            dma((SLOTS,)),
            pltpu.SMEM((2, SLOTS), jnp.int32),
            pltpu.VMEM((2, 1, PAIRS), jnp.int32),
            pltpu.VMEM((BANDS, POINTS), BF16),
            pltpu.VMEM((SIDE, CHUNKS, 2, BANDS, PART), BF16),
            pltpu.VMEM((2 * HALF_ROWS, 512), BF16),
            pltpu.VMEM((512, 256), BF16),
            pltpu.VMEM((512, PAIRS), BF16),
            pltpu.VMEM((CHUNKS, SIDE, STRIP, OWN_PAIRS), F32),
            pltpu.VMEM((CHUNKS, SIDE, STRIP, OWN_PAIRS), F32),
            pltpu.VMEM((CHUNKS, SIDE, STRIP, OWN_PAIRS), F32),
            pltpu.VMEM((CHUNKS, SIDE, STRIP, OWN_PAIRS), BF16),
            pltpu.VMEM((CHUNKS, SIDE - 1, STRIP, OWN_PAIRS), BF16),
            pltpu.VMEM((CHUNKS, STRIP, OWN_PAIRS), BF16),
            pltpu.VMEM((CHUNKS, STRIP, OWN_PAIRS), BF16),
            pltpu.VMEM((SIDE, SIDE, BANDS, PART), BF16),
            pltpu.VMEM((SIDE, SIDE, BANDS, PART), BF16),
            pltpu.VMEM((2, CHUNKS, SIDE, SIDE, STRIP, OWN_PAIRS), BF16),
            pltpu.VMEM((SIDE, 2, CHUNKS, SLOTS * BANDS, PART), BF16),
            pltpu.VMEM((CHUNKS, SLOTS * BANDS, PART), BF16),
            dma((6,)),
            dma((3,)),
            dma((3,)),
            dma((CHUNKS, 3)),
            dma((CHUNKS, 3)),
            dma((CHUNKS,)),
            dma((CHUNKS,)),
        ]
        + [dma((CHUNKS, 3)), dma((CHUNKS, 3)), dma((CHUNKS, 4)), dma((CHUNKS, 4))] * 2
        + [
            dma((CHUNKS, 4)),
            dma((CHUNKS, 4)),
            dma((CHUNKS, 2)),
            dma((CHUNKS, 2)),
            dma((CHUNKS, 2, 2)),
            dma((CHUNKS,)),
            dma((CHUNKS,)),
            dma((CHUNKS, 2)),
            dma((CHUNKS, 2)),
        ],
        compiler_params=pltpu.CompilerParams(
            collective_id=0, has_side_effects=True, vmem_limit_bytes=63 * 2**20
        ),
    )(
        partners.reshape(-1),
        first_band.reshape(1, -1),
        second_band.reshape(1, -1),
        screened,
        valence,
        conduction,
    )
    return kernel.reshape((1, 1) + kernel.shape)


def solution(mesh):
    in_specs = (
        P("cond", ("grp", "val")),
        P(("grp", "val"), None),
        P(),
        P(),
        P("cond", None),
        P("grp", "cond", None),
    )
    out_specs = P("grp", "cond", None, None, "val")
    return jax.shard_map(
        on_device, mesh=mesh, in_specs=in_specs, out_specs=out_specs, check_vma=False
    )
```

```python
import math

import jax
import jax.numpy as jnp
from jax import lax
from jax.experimental import pallas as pl
from jax.experimental.pallas import tpu as pltpu
from jax.sharding import PartitionSpec as P

MESH = pl.DeviceIdType.MESH
BF16 = jnp.bfloat16
F32 = jnp.float32
SIDE = 4
BANDS = 32
SLOTS = 4
POINTS = 8192
PAIRS = 512
OWN_PAIRS = 128
HALF_ROWS = 256
CHUNKS = 2
STRIP = HALF_ROWS // CHUNKS
QUARTER = POINTS // SIDE
PART = SIDE * STRIP


def whole_kernel(
    partners_ref,
    first_ref,
    second_ref,
    screened_ref,
    valence_ref,
    conduction_ref,
    final_ref,
    out_ref,
    out_sem,
    partners,
    bands,
    natural,
    left,
    scr,
    val,
    dens,
    pair_out,
    pair_in,
    sums,
    tosend,
    parts,
    zout,
    zin,
    gath_first,
    gath_second,
    mix,
    sel,
    sib,
    load_sem,
    pair_send,
    pair_recv,
    y_send,
    y_recv,
    z_send,
    z_recv,
    ga_send,
    ga_recv,
    gb_send,
    gb_recv,
    ma_send,
    ma_recv,
    mb_send,
    mb_recv,
    ms_send,
    ms_recv,
    own_send,
    other_send,
    near_recv,
    sib_send,
    sib_recv,
    relay_send,
    relay_recv,
):
    grp = lax.axis_index("grp")
    cond = lax.axis_index("cond")
    y = lax.axis_index("val")
    core = lax.rem(grp, 2)
    x = lax.rem(cond, SIDE)
    zlo = cond // SIDE
    z = (grp // 2) * SIDE + zlo
    par = lax.rem(x, 2)

    def device(px, py, pz, pcore):
        px = lax.rem(px + SIDE, SIDE)
        py = lax.rem(py + SIDE, SIDE)
        pz = lax.rem(pz + 2 * SIDE, 2 * SIDE)
        return ((pz // SIDE) * 2 + pcore, lax.rem(pz, SIDE) * SIDE + px, py)

    sibling = device(x, y, z, 1 - core)
    opposite = device(x, y, z + SIDE, core)

    def z_step(j, up):
        return (0, 1, up * 4 - 2, -1)[j]

    pa = x * (1 - core) + zlo * core
    pb = zlo * (1 - core) + x * core

    def peer_a(j):
        return device(x + j * (1 - core), y, z + z_step(j, par) * core, core)

    def peer_b(j, up):
        return device(x + j * core, y, z + z_step(j, up) * (1 - core), core)

    def back(p, j):
        return lax.rem(p + SIDE - j, SIDE)

    def remote(src, dst, ssem, rsem, dev):
        return pltpu.make_async_remote_copy(
            src_ref=src, dst_ref=dst, send_sem=ssem, recv_sem=rsem, device_id=dev,
            device_id_type=MESH,
        )

    copies = [
        (conduction_ref, natural),
        (first_ref, bands.at[0]),
        (second_ref, bands.at[1]),
        (valence_ref, val),
        (screened_ref, scr),
        (partners_ref, partners.at[0]),
    ]
    loads = [
        pltpu.make_async_copy(src, dst, load_sem.at[i]) for i, (src, dst) in enumerate(copies)
    ]
    load_natural, load_first, load_second, load_val, load_scr, load_partners = loads
    for load in loads:
        load.start()

    peers = [sibling, opposite]
    peers += [device(x, y + j, z, core) for j in (1, 2, 3)]
    peers += [device(x, y + j, z, 1 - core) for j in (1, 3)]
    peers += [device(x + j, y, z, core) for j in (1, 2, 3)]
    peers += [device(x, y, z + j, core) for j in (1, -1, 2, -2)]
    barrier = pltpu.get_barrier_semaphore()
    for peer in peers:
        pl.semaphore_signal(barrier, inc=1, device_id=peer, device_id_type=MESH)

    load_natural.wait()
    for q in range(SIDE):
        for t in range(CHUNKS):
            for h in range(2):
                for i in range(SIDE):
                    start = q * QUARTER + i * 2 * HALF_ROWS + h * HALF_ROWS + t * STRIP
                    left[q, t, h, :, i * STRIP : (i + 1) * STRIP] = natural[
                        :, start : start + STRIP
                    ]

    load_first.wait()
    load_second.wait()
    band = lax.broadcasted_iota(jnp.int32, (val.shape[1], PAIRS), 0)
    first_pick = jnp.where(band == bands[0], 1.0, 0.0).astype(BF16)
    second_pick = jnp.where(band == bands[1], 1.0, 0.0).astype(BF16)
    load_val.wait()
    for part in range(2):
        rows = pl.ds(part * 256, 256)
        points = val[rows, :]
        first_cols = jnp.dot(points, first_pick, preferred_element_type=F32)
        second_cols = jnp.dot(points, second_pick, preferred_element_type=F32)
        dens[rows, :] = (first_cols * second_cols).astype(BF16)
    load_scr.wait()
    for owner, kept in ((1 - core, pair_out), (core, sums)):
        for t in range(CHUNKS):
            start = pl.multiple_of(owner * HALF_ROWS + t * STRIP, STRIP)
            total = jnp.dot(scr[pl.ds(start, STRIP), :], dens[...], preferred_element_type=F32)
            for v in range(SIDE):
                kept[t, v] = total[:, v * OWN_PAIRS : (v + 1) * OWN_PAIRS]

    pl.semaphore_wait(barrier, len(peers))

    def pair_step(t):
        return remote(pair_out.at[t], pair_in.at[t], pair_send.at[t], pair_recv.at[t], sibling)

    give_partners = remote(
        partners_ref, partners.at[1], pair_send.at[CHUNKS], pair_recv.at[CHUNKS], sibling
    )
    for t in range(CHUNKS):
        pair_step(t).start()
    give_partners.start()

    low, high = pl.ds(0, 2), pl.ds(2, 2)

    class Gather:
        def __init__(self, buf, own, t, send_a, recv_a, send_b, recv_b):
            self.buf, self.own, self.t = buf, own, t
            self.send_a, self.recv_a, self.send_b, self.recv_b = send_a, recv_a, send_b, recv_b

        def step_a(self, j):
            sems = self.send_a.at[self.t, j - 1], self.recv_a.at[self.t, j - 1]
            return remote(self.own, self.buf.at[pb, pa], *sems, peer_a(j))

        def got_a(self, j):
            place = self.buf.at[pb, back(pa, j)]
            sems = self.send_a.at[self.t, j - 1], self.recv_a.at[self.t, j - 1]
            return remote(place, place, *sems, peer_a(j))

        def step_b(self, i):
            sems = self.send_b.at[self.t, i], self.recv_b.at[self.t, i]
            if i < 2:
                place = self.buf.at[pb]
                return remote(place, place, *sems, peer_b((1, 3)[i], 0))
            place = self.buf.at[pb, (low, high)[i - 2]]
            return remote(place, place, *sems, peer_b(2, i - 2))

        def got_b(self, i):
            sems = self.send_b.at[self.t, i], self.recv_b.at[self.t, i]
            if i < 2:
                place = self.buf.at[back(pb, (1, 3)[i])]
            else:
                place = self.buf.at[back(pb, 2), (low, high)[i - 2]]
            return remote(place, place, *sems, sibling)

        def start_a(self):
            for j in (2, 1, 3):
                self.step_a(j).start()

        def a_to_b(self):
            for j in (1, 3, 2):
                self.got_a(j).wait_recv()
            for i in (2, 3, 0, 1):
                self.step_b(i).start()

        def drain(self):
            for j in (1, 2, 3):
                self.step_a(j).wait_send()
            for i in range(4):
                self.step_b(i).wait_send()

    gath = (gath_first, gath_second)
    cond_gather = [
        Gather(gath[t], left.at[y, t, core], t, ga_send, ga_recv, gb_send, gb_recv)
        for t in range(CHUNKS)
    ]
    for t in range(CHUNKS):
        cond_gather[t].start_a()
        gath[t][pb, pa] = left[y, t, core]

    def y_step(j, t):
        return remote(
            tosend.at[t, lax.rem(y + j, SIDE)], parts.at[t, j - 1], y_send.at[t, j - 1],
            y_recv.at[t, j - 1], device(x, y + j, z, core),
        )

    for t in range(CHUNKS):
        pair_step(t).wait_recv()
        for v in range(SIDE):
            block = sums[t, v] + pair_in[t, v]
            sums[t, v] = block
            tosend[t, v] = block.astype(BF16)
        for j in (1, 3, 2):
            y_step(j, t).start()

    def z_copy(t):
        return remote(zout.at[t], zin.at[t], z_send.at[t], z_recv.at[t], opposite)

    for t in range(CHUNKS):
        for j in (1, 3, 2):
            y_step(j, t).wait_recv()
        summed = sums[t, y]
        for j in (1, 2, 3):
            summed += parts[t, j - 1].astype(F32)
        zout[t] = summed.astype(BF16)
        sums[t, 0] = summed
        z_copy(t).start()
    for t in range(CHUNKS):
        cond_gather[t].a_to_b()

    def own_step(j, t):
        place = sel.at[y, core, t]
        i = (j - 1) // 2
        return remote(
            place, place, own_send.at[t, i], near_recv.at[t, i, core], device(x, y + j, z, core)
        )

    def other_step(j, t):
        i = (j - 1) // 2
        return remote(
            sib.at[t], sel.at[y, core, t], other_send.at[t, i], near_recv.at[t, i, core],
            device(x, y + j, z, 1 - core),
        )

    def sib_step(t):
        return remote(sib.at[t], sel.at[y, core, t], sib_send.at[t], sib_recv.at[t], sibling)

    def near_got(j, h, t):
        place = sel.at[back(y, j), h, t]
        i = (j - 1) // 2
        return remote(place, place, own_send.at[t, i], near_recv.at[t, i, h], sibling)

    def relay_step(h, t):
        place = sel.at[back(y, (1, 3)[h]), h, t]
        return remote(
            place, place, relay_send.at[t, h], relay_recv.at[t, h],
            device(x, y + (1, 3)[h], z, core),
        )

    def relay(t):
        near_got(1, 0, t).wait_recv()
        relay_step(0, t).start()
        near_got(3, 1, t).wait_recv()
        relay_step(1, t).start()

    mix_gather = [
        Gather(mix.at[core, t], mix.at[core, t, pb, pa], t, ma_send, ma_recv, mb_send, mb_recv)
        for t in range(CHUNKS)
    ]

    def cross_step(i, t):
        place = mix.at[core, t, back(pb, (0, 1, 3, 2)[i])]
        return remote(place, place, ms_send.at[t, i], ms_recv.at[t, i], sibling)

    def cross_got(i, t):
        place = mix.at[1 - core, t, i]
        return remote(place, place, ms_send.at[t, i], ms_recv.at[t, i], sibling)

    def b_to_cross(t):
        for i in range(2):
            mix_gather[t].got_b(i).wait_recv()
            cross_step(i + 1, t).start()
        for i in range(2, 4):
            mix_gather[t].got_b(i).wait_recv()
        cross_step(3, t).start()

    def cross_all(t):
        for i in range(4):
            cross_got(i, t).wait_recv()

    for t in range(CHUNKS):
        z_copy(t).wait_recv()
        mix[core, t, pb, pa] = (sums[t, 0] + zin[t].astype(F32)).astype(BF16)
        mix_gather[t].start_a()
    out_ref[...] = jnp.zeros_like(out_ref)
    for t in range(CHUNKS):
        mix_gather[t].a_to_b()
        cross_step(0, t).start()
    load_partners.wait()
    give_partners.wait_recv()
    def pick_and_send(t):
        for i in range(4):
            cond_gather[t].got_b(i).wait_recv()
        for s in range(SLOTS):
            rows = pl.ds(s * BANDS, BANDS)
            for which in range(2):
                block = jnp.maximum(partners[which, s], 0)
                block_z = block // SIDE
                block_x = lax.rem(block, SIDE)
                picked = gath[t][
                    block_z * (1 - core) + block_x * core,
                    block_x * (1 - core) + block_z * core,
                ]
                if which == 0:
                    sel[y, core, t, rows, :] = picked
                else:
                    sib[t, rows, :] = picked
        for j in (1, 3):
            own_step(j, t).start()
            other_step(j, t).start()
        sib_step(t).start()

    pick_and_send(0)
    b_to_cross(0)
    pick_and_send(1)
    cross_all(0)

    def unit(u, carry):
        t = u // SIDE
        step = lax.rem(u, SIDE)
        ahead = step + step // 2 - 2 * (step // 3)
        q = lax.rem(y + ahead, SIDE)

        def arrived(h, sem):
            place = sel.at[q, h, t]
            remote(place, place, own_send.at[0, 0], sem, sibling).wait_recv()

        @pl.when(u == 1)
        def _():
            b_to_cross(1)
            relay(0)

        @pl.when(u == 3)
        def _():
            relay(1)

        @pl.when(step == 0)
        def _():
            arrived(1 - core, sib_recv.at[t])

        @pl.when(step == 1)
        def _():
            arrived(0, near_recv.at[t, 1, 0])

        @pl.when(step == 2)
        def _():
            arrived(1, near_recv.at[t, 0, 1])

        @pl.when(step == 3)
        def _():
            arrived(0, relay_recv.at[t, 0])
            arrived(1, relay_recv.at[t, 1])

        @pl.when(u == SIDE)
        def _():
            cross_all(1)

        mixed = jnp.concatenate(
            [mix[0, t, q, i] for i in range(SIDE)] + [mix[1, t, i, q] for i in range(SIDE)], 0
        )
        for s in range(SLOTS):
            rows = slice(s * BANDS, (s + 1) * BANDS)
            right = jnp.concatenate([sel[q, 0, t, rows, :], sel[q, 1, t, rows, :]], 1)
            blocks = []
            for i in range(BANDS):
                row = jnp.concatenate(
                    [left[q, t, 0, i : i + 1, :], left[q, t, 1, i : i + 1, :]], 1
                )
                blocks.append(jnp.broadcast_to(row, right.shape) * right)
            density = jnp.concatenate(blocks, 0)
            out_ref[s] += jnp.dot(density, mixed, preferred_element_type=F32)
        return carry

    lax.fori_loop(0, CHUNKS * SIDE, unit, 0)
    def write(s):
        return pltpu.make_async_copy(out_ref.at[s], final_ref.at[s], out_sem.at[s])

    for s in range(SLOTS):
        scale = jnp.where(partners[0, s] >= 0, 1.0 / math.sqrt(POINTS), 0.0)
        out_ref[s] = out_ref[s] * scale
        write(s).start()

    give_partners.wait_send()
    for t in range(CHUNKS):
        pair_step(t).wait_send()
        for j in (1, 2, 3):
            y_step(j, t).wait_send()
        z_copy(t).wait_send()
        for j in (1, 3):
            own_step(j, t).wait_send()
            other_step(j, t).wait_send()
        sib_step(t).wait_send()
        for h in range(2):
            relay_step(h, t).wait_send()
        for i in range(4):
            cross_step(i, t).wait_send()
        cond_gather[t].drain()
        mix_gather[t].drain()
    for s in range(SLOTS):
        write(s).wait()


def on_device(screened, valence, first_band, second_band, conduction, partners):
    vmem = pl.BlockSpec(memory_space=pltpu.VMEM)
    hbm = pl.BlockSpec(memory_space=pltpu.HBM)
    dma = pltpu.SemaphoreType.DMA
    kernel = pl.pallas_call(
        whole_kernel,
        out_shape=jax.ShapeDtypeStruct((SLOTS, BANDS * BANDS, OWN_PAIRS), F32),
        in_specs=[hbm] * 6,
        out_specs=hbm,
        scratch_shapes=[
            pltpu.VMEM((SLOTS, BANDS * BANDS, OWN_PAIRS), F32),
            dma((SLOTS,)),
            pltpu.SMEM((2, SLOTS), jnp.int32),
            pltpu.VMEM((2, 1, PAIRS), jnp.int32),
            pltpu.VMEM((BANDS, POINTS), BF16),
            pltpu.VMEM((SIDE, CHUNKS, 2, BANDS, PART), BF16),
            pltpu.VMEM((2 * HALF_ROWS, 512), BF16),
            pltpu.VMEM((512, 256), BF16),
            pltpu.VMEM((512, PAIRS), BF16),
            pltpu.VMEM((CHUNKS, SIDE, STRIP, OWN_PAIRS), F32),
            pltpu.VMEM((CHUNKS, SIDE, STRIP, OWN_PAIRS), F32),
            pltpu.VMEM((CHUNKS, SIDE, STRIP, OWN_PAIRS), F32),
            pltpu.VMEM((CHUNKS, SIDE, STRIP, OWN_PAIRS), BF16),
            pltpu.VMEM((CHUNKS, SIDE - 1, STRIP, OWN_PAIRS), BF16),
            pltpu.VMEM((CHUNKS, STRIP, OWN_PAIRS), BF16),
            pltpu.VMEM((CHUNKS, STRIP, OWN_PAIRS), BF16),
            pltpu.VMEM((SIDE, SIDE, BANDS, PART), BF16),
            pltpu.VMEM((SIDE, SIDE, BANDS, PART), BF16),
            pltpu.VMEM((2, CHUNKS, SIDE, SIDE, STRIP, OWN_PAIRS), BF16),
            pltpu.VMEM((SIDE, 2, CHUNKS, SLOTS * BANDS, PART), BF16),
            pltpu.VMEM((CHUNKS, SLOTS * BANDS, PART), BF16),
            dma((6,)),
            dma((3,)),
            dma((3,)),
            dma((CHUNKS, 3)),
            dma((CHUNKS, 3)),
            dma((CHUNKS,)),
            dma((CHUNKS,)),
        ]
        + [dma((CHUNKS, 3)), dma((CHUNKS, 3)), dma((CHUNKS, 4)), dma((CHUNKS, 4))] * 2
        + [
            dma((CHUNKS, 4)),
            dma((CHUNKS, 4)),
            dma((CHUNKS, 2)),
            dma((CHUNKS, 2)),
            dma((CHUNKS, 2, 2)),
            dma((CHUNKS,)),
            dma((CHUNKS,)),
            dma((CHUNKS, 2)),
            dma((CHUNKS, 2)),
        ],
        compiler_params=pltpu.CompilerParams(
            collective_id=0, has_side_effects=True, vmem_limit_bytes=63 * 2**20
        ),
    )(
        partners.reshape(-1),
        first_band.reshape(1, -1),
        second_band.reshape(1, -1),
        screened,
        valence,
        conduction,
    )
    return kernel.reshape((1, 1) + kernel.shape)


def solution(mesh):
    in_specs = (
        P("cond", ("grp", "val")),
        P(("grp", "val"), None),
        P(),
        P(),
        P("cond", None),
        P("grp", "cond", None),
    )
    out_specs = P("grp", "cond", None, None, "val")
    return jax.shard_map(
        on_device, mesh=mesh, in_specs=in_specs, out_specs=out_specs, check_vma=False
    )
```

```python
import math

import jax
import jax.numpy as jnp
from jax import lax
from jax.experimental import pallas as pl
from jax.experimental.pallas import tpu as pltpu
from jax.sharding import PartitionSpec as P

MESH = pl.DeviceIdType.MESH
BF16 = jnp.bfloat16
F32 = jnp.float32
SIDE = 4
BANDS = 32
SLOTS = 4
POINTS = 8192
PAIRS = 512
OWN_PAIRS = 128
HALF_ROWS = 256
CHUNKS = 2
STRIP = HALF_ROWS // CHUNKS
QUARTER = POINTS // SIDE
PART = SIDE * STRIP


def whole_kernel(
    partners_ref,
    first_ref,
    second_ref,
    screened_ref,
    valence_ref,
    conduction_ref,
    final_ref,
    out_ref,
    out_sem,
    partners,
    bands,
    natural,
    left,
    scr,
    val,
    dens,
    pair_out,
    pair_in,
    sums,
    tosend,
    parts,
    zout,
    zin,
    gath_first,
    gath_second,
    mix,
    sel,
    sib,
    load_sem,
    pair_send,
    pair_recv,
    y_send,
    y_recv,
    z_send,
    z_recv,
    ga_send,
    ga_recv,
    gb_send,
    gb_recv,
    ma_send,
    ma_recv,
    mb_send,
    mb_recv,
    ms_send,
    ms_recv,
    own_send,
    other_send,
    near_recv,
    sib_send,
    sib_recv,
    relay_send,
    relay_recv,
):
    grp = lax.axis_index("grp")
    cond = lax.axis_index("cond")
    y = lax.axis_index("val")
    core = lax.rem(grp, 2)
    x = lax.rem(cond, SIDE)
    zlo = cond // SIDE
    z = (grp // 2) * SIDE + zlo
    par = lax.rem(x, 2)

    def device(px, py, pz, pcore):
        px = lax.rem(px + SIDE, SIDE)
        py = lax.rem(py + SIDE, SIDE)
        pz = lax.rem(pz + 2 * SIDE, 2 * SIDE)
        return ((pz // SIDE) * 2 + pcore, lax.rem(pz, SIDE) * SIDE + px, py)

    sibling = device(x, y, z, 1 - core)
    opposite = device(x, y, z + SIDE, core)

    def z_step(j, up):
        return (0, 1, up * 4 - 2, -1)[j]

    pa = x * (1 - core) + zlo * core
    pb = zlo * (1 - core) + x * core

    def peer_a(j):
        return device(x + j * (1 - core), y, z + z_step(j, par) * core, core)

    def peer_b(j, up):
        return device(x + j * core, y, z + z_step(j, up) * (1 - core), core)

    def back(p, j):
        return lax.rem(p + SIDE - j, SIDE)

    def remote(src, dst, ssem, rsem, dev):
        return pltpu.make_async_remote_copy(
            src_ref=src, dst_ref=dst, send_sem=ssem, recv_sem=rsem, device_id=dev,
            device_id_type=MESH,
        )

    copies = [
        (conduction_ref, natural),
        (first_ref, bands.at[0]),
        (second_ref, bands.at[1]),
        (valence_ref, val),
        (screened_ref, scr),
        (partners_ref, partners.at[0]),
    ]
    loads = [
        pltpu.make_async_copy(src, dst, load_sem.at[i]) for i, (src, dst) in enumerate(copies)
    ]
    load_natural, load_first, load_second, load_val, load_scr, load_partners = loads
    for load in loads:
        load.start()

    peers = [sibling, opposite]
    peers += [device(x, y + j, z, core) for j in (1, 2, 3)]
    peers += [device(x, y + j, z, 1 - core) for j in (1, 3)]
    peers += [device(x + j, y, z, core) for j in (1, 2, 3)]
    peers += [device(x, y, z + j, core) for j in (1, -1, 2, -2)]
    barrier = pltpu.get_barrier_semaphore()
    for peer in peers:
        pl.semaphore_signal(barrier, inc=1, device_id=peer, device_id_type=MESH)

    load_natural.wait()
    for q in range(SIDE):
        for t in range(CHUNKS):
            for h in range(2):
                for i in range(SIDE):
                    start = q * QUARTER + i * 2 * HALF_ROWS + h * HALF_ROWS + t * STRIP
                    left[q, t, h, :, i * STRIP : (i + 1) * STRIP] = natural[
                        :, start : start + STRIP
                    ]

    load_first.wait()
    load_second.wait()
    band = lax.broadcasted_iota(jnp.int32, (val.shape[1], PAIRS), 0)
    first_pick = jnp.where(band == bands[0], 1.0, 0.0).astype(BF16)
    second_pick = jnp.where(band == bands[1], 1.0, 0.0).astype(BF16)
    load_val.wait()
    for part in range(2):
        rows = pl.ds(part * 256, 256)
        points = val[rows, :]
        first_cols = jnp.dot(points, first_pick, preferred_element_type=F32)
        second_cols = jnp.dot(points, second_pick, preferred_element_type=F32)
        dens[rows, :] = (first_cols * second_cols).astype(BF16)
    load_scr.wait()
    for owner, kept in ((1 - core, pair_out), (core, sums)):
        for t in range(CHUNKS):
            start = pl.multiple_of(owner * HALF_ROWS + t * STRIP, STRIP)
            total = jnp.dot(scr[pl.ds(start, STRIP), :], dens[...], preferred_element_type=F32)
            for v in range(SIDE):
                kept[t, v] = total[:, v * OWN_PAIRS : (v + 1) * OWN_PAIRS]

    pl.semaphore_wait(barrier, len(peers))

    def pair_step(t):
        return remote(pair_out.at[t], pair_in.at[t], pair_send.at[t], pair_recv.at[t], sibling)

    give_partners = remote(
        partners_ref, partners.at[1], pair_send.at[CHUNKS], pair_recv.at[CHUNKS], sibling
    )
    for t in range(CHUNKS):
        pair_step(t).start()
    give_partners.start()

    low, high = pl.ds(0, 2), pl.ds(2, 2)

    class Gather:
        def __init__(self, buf, own, t, send_a, recv_a, send_b, recv_b):
            self.buf, self.own, self.t = buf, own, t
            self.send_a, self.recv_a, self.send_b, self.recv_b = send_a, recv_a, send_b, recv_b

        def step_a(self, j):
            sems = self.send_a.at[self.t, j - 1], self.recv_a.at[self.t, j - 1]
            return remote(self.own, self.buf.at[pb, pa], *sems, peer_a(j))

        def got_a(self, j):
            place = self.buf.at[pb, back(pa, j)]
            sems = self.send_a.at[self.t, j - 1], self.recv_a.at[self.t, j - 1]
            return remote(place, place, *sems, peer_a(j))

        def step_b(self, i):
            sems = self.send_b.at[self.t, i], self.recv_b.at[self.t, i]
            if i < 2:
                place = self.buf.at[pb]
                return remote(place, place, *sems, peer_b((1, 3)[i], 0))
            place = self.buf.at[pb, (low, high)[i - 2]]
            return remote(place, place, *sems, peer_b(2, i - 2))

        def got_b(self, i):
            sems = self.send_b.at[self.t, i], self.recv_b.at[self.t, i]
            if i < 2:
                place = self.buf.at[back(pb, (1, 3)[i])]
            else:
                place = self.buf.at[back(pb, 2), (low, high)[i - 2]]
            return remote(place, place, *sems, sibling)

        def start_a(self):
            for j in (2, 1, 3):
                self.step_a(j).start()

        def a_to_b(self):
            for j in (1, 3, 2):
                self.got_a(j).wait_recv()
            for i in (2, 3, 0, 1):
                self.step_b(i).start()

        def drain(self):
            for j in (1, 2, 3):
                self.step_a(j).wait_send()
            for i in range(4):
                self.step_b(i).wait_send()

    gath = (gath_first, gath_second)
    cond_gather = [
        Gather(gath[t], left.at[y, t, core], t, ga_send, ga_recv, gb_send, gb_recv)
        for t in range(CHUNKS)
    ]
    for t in range(CHUNKS):
        cond_gather[t].start_a()
        gath[t][pb, pa] = left[y, t, core]

    def y_step(j, t):
        return remote(
            tosend.at[t, lax.rem(y + j, SIDE)], parts.at[t, j - 1], y_send.at[t, j - 1],
            y_recv.at[t, j - 1], device(x, y + j, z, core),
        )

    for t in range(CHUNKS):
        pair_step(t).wait_recv()
        for v in range(SIDE):
            block = sums[t, v] + pair_in[t, v]
            sums[t, v] = block
            tosend[t, v] = block.astype(BF16)
        for j in (1, 3, 2):
            y_step(j, t).start()

    def z_copy(t):
        return remote(zout.at[t], zin.at[t], z_send.at[t], z_recv.at[t], opposite)

    for t in range(CHUNKS):
        for j in (1, 3, 2):
            y_step(j, t).wait_recv()
        summed = sums[t, y]
        for j in (1, 2, 3):
            summed += parts[t, j - 1].astype(F32)
        zout[t] = summed.astype(BF16)
        sums[t, 0] = summed
        z_copy(t).start()
    for t in range(CHUNKS):
        cond_gather[t].a_to_b()

    def own_step(j, t):
        place = sel.at[y, core, t]
        i = (j - 1) // 2
        return remote(
            place, place, own_send.at[t, i], near_recv.at[t, i, core], device(x, y + j, z, core)
        )

    def other_step(j, t):
        i = (j - 1) // 2
        return remote(
            sib.at[t], sel.at[y, core, t], other_send.at[t, i], near_recv.at[t, i, core],
            device(x, y + j, z, 1 - core),
        )

    def sib_step(t):
        return remote(sib.at[t], sel.at[y, core, t], sib_send.at[t], sib_recv.at[t], sibling)

    def near_got(j, h, t):
        place = sel.at[back(y, j), h, t]
        i = (j - 1) // 2
        return remote(place, place, own_send.at[t, i], near_recv.at[t, i, h], sibling)

    def relay_step(h, t):
        place = sel.at[back(y, (1, 3)[h]), h, t]
        return remote(
            place, place, relay_send.at[t, h], relay_recv.at[t, h],
            device(x, y + (1, 3)[h], z, core),
        )

    def relay(t):
        near_got(1, 0, t).wait_recv()
        relay_step(0, t).start()
        near_got(3, 1, t).wait_recv()
        relay_step(1, t).start()

    mix_gather = [
        Gather(mix.at[core, t], mix.at[core, t, pb, pa], t, ma_send, ma_recv, mb_send, mb_recv)
        for t in range(CHUNKS)
    ]

    def cross_step(i, t):
        place = mix.at[core, t, back(pb, (0, 1, 3, 2)[i])]
        return remote(place, place, ms_send.at[t, i], ms_recv.at[t, i], sibling)

    def cross_got(i, t):
        place = mix.at[1 - core, t, i]
        return remote(place, place, ms_send.at[t, i], ms_recv.at[t, i], sibling)

    def b_to_cross(t):
        for i in range(2):
            mix_gather[t].got_b(i).wait_recv()
            cross_step(i + 1, t).start()
        for i in range(2, 4):
            mix_gather[t].got_b(i).wait_recv()
        cross_step(3, t).start()

    def cross_all(t):
        for i in range(4):
            cross_got(i, t).wait_recv()

    for t in range(CHUNKS):
        z_copy(t).wait_recv()
        mix[core, t, pb, pa] = (sums[t, 0] + zin[t].astype(F32)).astype(BF16)
        mix_gather[t].start_a()
    out_ref[...] = jnp.zeros_like(out_ref)
    for t in range(CHUNKS):
        mix_gather[t].a_to_b()
        cross_step(0, t).start()
    load_partners.wait()
    give_partners.wait_recv()
    def pick_and_send(t):
        for i in range(4):
            cond_gather[t].got_b(i).wait_recv()
        for s in range(SLOTS):
            rows = pl.ds(s * BANDS, BANDS)
            for which in range(2):
                block = jnp.maximum(partners[which, s], 0)
                block_z = block // SIDE
                block_x = lax.rem(block, SIDE)
                picked = gath[t][
                    block_z * (1 - core) + block_x * core,
                    block_x * (1 - core) + block_z * core,
                ]
                if which == 0:
                    sel[y, core, t, rows, :] = picked
                else:
                    sib[t, rows, :] = picked
        for j in (1, 3):
            own_step(j, t).start()
            other_step(j, t).start()
        sib_step(t).start()

    pick_and_send(0)
    b_to_cross(0)
    pick_and_send(1)
    cross_all(0)

    def unit(u, carry):
        t = u // SIDE
        step = lax.rem(u, SIDE)
        ahead = step + step // 2 - 2 * (step // 3)
        q = lax.rem(y + ahead, SIDE)

        def arrived(h, sem):
            place = sel.at[q, h, t]
            remote(place, place, own_send.at[0, 0], sem, sibling).wait_recv()

        @pl.when(u == 1)
        def _():
            b_to_cross(1)
            relay(0)

        @pl.when(u == SIDE)
        def _():
            relay(1)

        @pl.when(step == 0)
        def _():
            arrived(1 - core, sib_recv.at[t])

        @pl.when(step == 1)
        def _():
            arrived(0, near_recv.at[t, 1, 0])

        @pl.when(step == 2)
        def _():
            arrived(1, near_recv.at[t, 0, 1])

        @pl.when(step == 3)
        def _():
            arrived(0, relay_recv.at[t, 0])
            arrived(1, relay_recv.at[t, 1])

        @pl.when(u == SIDE)
        def _():
            cross_all(1)

        mixed = jnp.concatenate(
            [mix[0, t, q, i] for i in range(SIDE)] + [mix[1, t, i, q] for i in range(SIDE)], 0
        )
        for s in range(SLOTS):
            rows = slice(s * BANDS, (s + 1) * BANDS)
            right = jnp.concatenate([sel[q, 0, t, rows, :], sel[q, 1, t, rows, :]], 1)
            blocks = []
            for i in range(BANDS):
                row = jnp.concatenate(
                    [left[q, t, 0, i : i + 1, :], left[q, t, 1, i : i + 1, :]], 1
                )
                blocks.append(jnp.broadcast_to(row, right.shape) * right)
            density = jnp.concatenate(blocks, 0)
            out_ref[s] += jnp.dot(density, mixed, preferred_element_type=F32)
        return carry

    lax.fori_loop(0, CHUNKS * SIDE, unit, 0)
    def write(s):
        return pltpu.make_async_copy(out_ref.at[s], final_ref.at[s], out_sem.at[s])

    for s in range(SLOTS):
        scale = jnp.where(partners[0, s] >= 0, 1.0 / math.sqrt(POINTS), 0.0)
        out_ref[s] = out_ref[s] * scale
        write(s).start()

    give_partners.wait_send()
    for t in range(CHUNKS):
        pair_step(t).wait_send()
        for j in (1, 2, 3):
            y_step(j, t).wait_send()
        z_copy(t).wait_send()
        for j in (1, 3):
            own_step(j, t).wait_send()
            other_step(j, t).wait_send()
        sib_step(t).wait_send()
        for h in range(2):
            relay_step(h, t).wait_send()
        for i in range(4):
            cross_step(i, t).wait_send()
        cond_gather[t].drain()
        mix_gather[t].drain()
    for s in range(SLOTS):
        write(s).wait()


def on_device(screened, valence, first_band, second_band, conduction, partners):
    vmem = pl.BlockSpec(memory_space=pltpu.VMEM)
    hbm = pl.BlockSpec(memory_space=pltpu.HBM)
    dma = pltpu.SemaphoreType.DMA
    kernel = pl.pallas_call(
        whole_kernel,
        out_shape=jax.ShapeDtypeStruct((SLOTS, BANDS * BANDS, OWN_PAIRS), F32),
        in_specs=[hbm] * 6,
        out_specs=hbm,
        scratch_shapes=[
            pltpu.VMEM((SLOTS, BANDS * BANDS, OWN_PAIRS), F32),
            dma((SLOTS,)),
            pltpu.SMEM((2, SLOTS), jnp.int32),
            pltpu.VMEM((2, 1, PAIRS), jnp.int32),
            pltpu.VMEM((BANDS, POINTS), BF16),
            pltpu.VMEM((SIDE, CHUNKS, 2, BANDS, PART), BF16),
            pltpu.VMEM((2 * HALF_ROWS, 512), BF16),
            pltpu.VMEM((512, 256), BF16),
            pltpu.VMEM((512, PAIRS), BF16),
            pltpu.VMEM((CHUNKS, SIDE, STRIP, OWN_PAIRS), F32),
            pltpu.VMEM((CHUNKS, SIDE, STRIP, OWN_PAIRS), F32),
            pltpu.VMEM((CHUNKS, SIDE, STRIP, OWN_PAIRS), F32),
            pltpu.VMEM((CHUNKS, SIDE, STRIP, OWN_PAIRS), BF16),
            pltpu.VMEM((CHUNKS, SIDE - 1, STRIP, OWN_PAIRS), BF16),
            pltpu.VMEM((CHUNKS, STRIP, OWN_PAIRS), BF16),
            pltpu.VMEM((CHUNKS, STRIP, OWN_PAIRS), BF16),
            pltpu.VMEM((SIDE, SIDE, BANDS, PART), BF16),
            pltpu.VMEM((SIDE, SIDE, BANDS, PART), BF16),
            pltpu.VMEM((2, CHUNKS, SIDE, SIDE, STRIP, OWN_PAIRS), BF16),
            pltpu.VMEM((SIDE, 2, CHUNKS, SLOTS * BANDS, PART), BF16),
            pltpu.VMEM((CHUNKS, SLOTS * BANDS, PART), BF16),
            dma((6,)),
            dma((3,)),
            dma((3,)),
            dma((CHUNKS, 3)),
            dma((CHUNKS, 3)),
            dma((CHUNKS,)),
            dma((CHUNKS,)),
        ]
        + [dma((CHUNKS, 3)), dma((CHUNKS, 3)), dma((CHUNKS, 4)), dma((CHUNKS, 4))] * 2
        + [
            dma((CHUNKS, 4)),
            dma((CHUNKS, 4)),
            dma((CHUNKS, 2)),
            dma((CHUNKS, 2)),
            dma((CHUNKS, 2, 2)),
            dma((CHUNKS,)),
            dma((CHUNKS,)),
            dma((CHUNKS, 2)),
            dma((CHUNKS, 2)),
        ],
        compiler_params=pltpu.CompilerParams(
            collective_id=0, has_side_effects=True, vmem_limit_bytes=63 * 2**20
        ),
    )(
        partners.reshape(-1),
        first_band.reshape(1, -1),
        second_band.reshape(1, -1),
        screened,
        valence,
        conduction,
    )
    return kernel.reshape((1, 1) + kernel.shape)


def solution(mesh):
    in_specs = (
        P("cond", ("grp", "val")),
        P(("grp", "val"), None),
        P(),
        P(),
        P("cond", None),
        P("grp", "cond", None),
    )
    out_specs = P("grp", "cond", None, None, "val")
    return jax.shard_map(
        on_device, mesh=mesh, in_specs=in_specs, out_specs=out_specs, check_vma=False
    )
```
